256 devices in a mesh: segment: 2 (over core), latent: 16 (over y, x), dp: 8 (over z).
Axes of the slice: x: 4, y: 4, z: 8, core: 2. Of those that a mesh axis runs over, the one named last changes fastest.
Arguments:
- resid_in: bfloat16 [4, 128, 3584], P(None, 'dp', 'latent'), may hold values from -40 to 40
- norm_gain: float32 [2, 3584], P('segment'), may hold values from 0.25 to 1.75
- enc_weight: bfloat16 [2, 3584, 65536], P('segment', None, ('latent', 'dp')), may hold values from -0.09375 to 0.09375
- enc_bias: float32 [2, 65536], P('segment', ('latent', 'dp')), may hold values from -3 to 3
- dec_self: bfloat16 [2, 65536, 3584], P('segment', ('latent', 'dp')), may hold values from -0.25 to 0.25
- dec_cross: bfloat16 [65536, 3584], P(('latent', 'dp')), may hold values from -0.25 to 0.25
- block_ids: int32 [2, 4, 2, 128, 4], P('segment', None, None, ('latent', 'dp')), may hold values from 0 to 7, as said below
- block_counts: int32 [2, 4, 2, 128], P('segment', None, None, ('latent', 'dp')), may hold values from 1 to 4, as said below
Outputs:
- recon: bfloat16 [2, 4, 128, 3584], P('segment', None, 'dp', 'latent')
The draws below stay inside these ranges and needn't reach their ends.
Inputs may be any that keep to these rules, and one draw needn't show every extreme that they name: `block_ids`: the 4 entries of one list are distinct local block numbers. `block_counts`: in every tile of every layer and micro-batch some device group has 4 live blocks.
All inputs are finite; a program needn't handle non-finite values.
Results may differ from the reference program's by a relative error of at most 0.007.
Values may be sent and summed in bfloat16 or wider, within the bound.
No kernel may reach another device: no remote copies, remote signals or barrier semaphores. Data moves between devices by JAX's collectives and lax.ppermute only.
A program may use at most 64 MiB of HBM per device.

```python
import math
import jax
import jax.numpy as jnp
from jax import lax

D = 3584
BLK_DEV = 8
BLOCK = 64
CAP = 4
TILE = 64
MB = 4
LAYERS = 2
TOKENS = 128
TILES = 2
GROUPS = 128
LATENTS = 65536


def draw_resid_in(key, part):
    key = jax.random.fold_in(key, 5)
    key_rows, key_cols, key_base = jax.random.split(key, 3)
    half_decade = 0.5 * math.log(10.0)
    row_scale = jnp.exp(jax.random.uniform(key_rows, (MB, TOKENS, 1), jnp.float32, -half_decade, half_decade))
    col_scale = jnp.exp(jax.random.uniform(key_cols, (1, 1, D), jnp.float32, -half_decade, half_decade))
    base = jax.random.truncated_normal(key_base, -4.0, 4.0, (MB, TOKENS, D), jnp.float32)
    return (base * row_scale * col_scale).astype(jnp.bfloat16)


def draw_block_ids(key, part):
    key = jax.random.fold_in(key, 7)
    scores = jax.random.randint(key, (LAYERS, MB, TILES, GROUPS, BLK_DEV), 0, 65536, jnp.int32)
    scores = scores * BLK_DEV + jnp.arange(BLK_DEV, dtype=jnp.int32)
    ordering = jnp.argsort(scores, axis=-1)
    return ordering[..., :CAP].astype(jnp.int32)


def draw_block_counts(key, part):
    key = jax.random.fold_in(key, 11)
    key_high, key_pick, key_full = jax.random.split(key, 3)
    ceiling = jax.random.randint(key_high, (LAYERS, 1, 1, GROUPS), 1, CAP + 1, jnp.int32)
    raw_values = jax.random.randint(key_pick, (LAYERS, MB, TILES, GROUPS), 0, 1048576, jnp.int32)
    counts = 1 + raw_values % ceiling
    chosen = jax.random.randint(key_full, (LAYERS, MB, TILES, 1), 0, GROUPS, jnp.int32)
    counts = jnp.where(jnp.arange(GROUPS, dtype=jnp.int32) == chosen, CAP, counts)
    return counts.astype(jnp.int32)


def with_spikes(drawn, rng, source, target, shards_of, factor):
    owner, partner = [(jnp.arange(drawn.shape[position]) // (drawn.shape[position] // shards_of)).reshape([-1 if axis == position else 1 for axis in range(drawn.ndim)]) for position in (source, target)]
    chosen = jax.random.permutation(rng, shards_of)[partner]
    strong = (owner == chosen) | (owner == (partner + shards_of // 2) % shards_of)
    return jnp.where(strong, factor * drawn, drawn)


def block_scale(stream_key, shape, cuts, smallest, high):
    def one(position, parts):
        heights = jax.random.uniform(jax.random.fold_in(jax.random.fold_in(stream_key, 6), position), (parts,), jnp.float32, smallest / len(cuts), high / len(cuts))
        return jnp.repeat(jnp.exp(heights), shape[position] // parts).reshape((-1,) + (1,) * (len(shape) - position - 1))

    loudness = one(*cuts[0])
    for cut in cuts[1:]:
        loudness = loudness * one(*cut)
    return loudness


def centred(stream_key, shape, deviation, most, cuts=(), kind=jnp.bfloat16):
    array = jax.random.normal(stream_key, shape, jnp.float32) * deviation
    if len(cuts) > 0:
        array = block_scale(stream_key, shape, cuts, -0.22, 0.18) * array
    return jnp.clip(array, min=-most, max=most).astype(kind)


def gaussian_with(key, dims, spread, most, pieces, heavy, held_as=jnp.bfloat16):
    result = spread * jax.random.normal(key, dims, jnp.float32)
    if pieces:
        result = result * block_scale(key, dims, pieces, -0.22, 0.18)
    return jnp.clip(with_spikes(result, jax.random.fold_in(key, 3), *heavy), -most, most).astype(held_as)


def setup_inputs(seed: int = 0) -> dict:
    seeds = jax.random.split(jax.random.key(seed), 9)
    resid_in = draw_resid_in(jax.random.fold_in(seeds[8], 71), 0)
    norm_gain = jnp.clip(1.0 + 0.15 * jax.random.normal(seeds[1], (LAYERS, D), jnp.float32), 0.25, 1.75)
    enc_weight = centred(seeds[2], (LAYERS, D, LATENTS), D ** -0.5, 0.09375, ((0, 2), (2, 128)))
    enc_bias = centred(seeds[3], (LAYERS, LATENTS), 0.5, 3.0, ((0, 2), (1, 128)), jnp.float32)
    dec_self = gaussian_with(seeds[4], (LAYERS, LATENTS, D), (LATENTS // 8) ** -0.5, 0.25, ((0, 2), (1, 128)), (1, 2, 128, 5.5))
    dec_cross = gaussian_with(seeds[5], (LATENTS, D), (LATENTS // 8) ** -0.5, 0.25, ((0, 128),), (0, 1, 128, 5.5))
    block_ids = draw_block_ids(jax.random.fold_in(seeds[8], 71), 0)
    block_counts = draw_block_counts(jax.random.fold_in(seeds[8], 71), 0)
    return dict(resid_in=resid_in, norm_gain=norm_gain, enc_weight=enc_weight, enc_bias=enc_bias, dec_self=dec_self, dec_cross=dec_cross, block_ids=block_ids, block_counts=block_counts)


norm_eps = 1e-06

def normalize(resid, gain_row):
    values = resid.astype(jnp.float32)
    scaling = lax.rsqrt(lax.optimization_barrier(jnp.mean(values * values, axis=-1, keepdims=True)) + norm_eps)
    return (values * scaling * gain_row.astype(jnp.float32)).astype(jnp.bfloat16)

def live_mask(list_ids, list_counts):
    slot_live = jnp.arange(CAP, dtype=jnp.int32) < list_counts[..., None]
    matches = (list_ids[..., None] == jnp.arange(BLK_DEV, dtype=jnp.int32)) & slot_live[..., None]
    return jnp.any(matches, axis=2).astype(jnp.float32)

def encode(resid, gain_row, weights, biases, list_ids, list_counts):
    normed = normalize(resid, gain_row)
    before = jnp.dot(normed, weights, preferred_element_type=jnp.float32) + biases.astype(jnp.float32)
    before = before.reshape(TILES, TILE, GROUPS, BLK_DEV, BLOCK)
    active = jnp.maximum(before, 0.0) * live_mask(list_ids, list_counts)[:, None, :, :, None]
    return active.reshape(TOKENS, LATENTS).astype(jnp.bfloat16)

def reference(resid_in, norm_gain, enc_weight, enc_bias, dec_self, dec_cross, block_ids, block_counts):
    results = []
    for batch_index in range(MB):
        resid = resid_in[batch_index]
        earlier = jnp.zeros((TOKENS, LATENTS), jnp.bfloat16)
        layer_outs = []
        for layer_index in range(LAYERS):
            active = encode(resid, norm_gain[layer_index], enc_weight[layer_index], enc_bias[layer_index], block_ids[layer_index, batch_index], block_counts[layer_index, batch_index])
            total = jnp.dot(active, dec_self[layer_index], preferred_element_type=jnp.float32)
            if layer_index > 0:
                total = total + jnp.dot(earlier, dec_cross, preferred_element_type=jnp.float32)
            output = total.astype(jnp.bfloat16)
            layer_outs.append(output)
            resid = (resid.astype(jnp.float32) + output.astype(jnp.float32)).astype(jnp.bfloat16)
            earlier = active
        results.append(jnp.stack(layer_outs))
    return jnp.stack(results, axis=1)
```

```python
import jax
import jax.numpy as jnp
from jax import lax
from jax.sharding import PartitionSpec as P

BLK_DEV = 8
BLOCK = 64

norm_eps = 1e-06


def swapped(value):
    return lax.ppermute(value, "segment", [(0, 1), (1, 0)])


def exchanged(value, axis):
    return lax.all_to_all(value, axis, 0, 0)


def spread(value, axis):
    count = lax.axis_size(axis)
    return exchanged(jnp.broadcast_to(value[None], (count,) + value.shape), axis)


def normalize(resid, gain_row):
    values = resid.astype(jnp.float32)
    scaling = lax.rsqrt(jnp.mean(values * values, axis=-1, keepdims=True) + norm_eps)
    return (values * scaling * gain_row).astype(jnp.bfloat16)


def summed(parts):
    return jnp.sum(parts.astype(jnp.float32), axis=0).astype(jnp.bfloat16)


def body(resid_in, norm_gain, enc_weight, enc_bias, dec_self, dec_cross, block_ids, block_counts):
    segment_index = lax.axis_index("segment")
    is_first = segment_index == 0
    latents = lax.axis_size("latent")
    dps = lax.axis_size("dp")
    batches, own_rows, own_cols = resid_in.shape
    half = batches // 2
    cols = latents * own_cols
    width = enc_weight.shape[2]
    pair = half * own_rows // latents
    rows = half * own_rows * dps

    list_ids = block_ids[0, :, :, 0, :]
    counts = block_counts[0, :, :, 0]
    slot_live = jnp.arange(list_ids.shape[-1], dtype=jnp.int32) < counts[..., None]
    matches = (list_ids[..., None] == jnp.arange(BLK_DEV, dtype=jnp.int32)) & slot_live[..., None]
    live_own = jnp.any(matches, axis=2).astype(jnp.float32)
    tiles = live_own.shape[1]

    small_own = jnp.concatenate([norm_gain[0], enc_bias[0], live_own.reshape(-1)])
    enc_other = swapped(enc_weight[0])
    dec_other = swapped(dec_self[0])
    small_other = swapped(small_own)

    def layered(own, other):
        return jnp.where(is_first, own, other), jnp.where(is_first, other, own)

    enc = layered(enc_weight[0], enc_other)
    dec = layered(dec_self[0], dec_other)
    small = layered(small_own, small_other)

    def parts_of(values):
        gain = values[:cols]
        bias = values[cols : cols + width]
        live = values[cols + width :].reshape(batches, tiles, BLK_DEV)
        live = lax.dynamic_slice_in_dim(live, segment_index * half, half, 0)
        live = jnp.broadcast_to(
            live[:, None, :, None, :, None],
            (half, latents // half, tiles, dps // tiles * pair, BLK_DEV, BLOCK),
        )
        return gain, bias, live.reshape(rows, width)

    def encode(normed, layer):
        _, bias, live = parts_of(small[layer])
        before = jnp.dot(normed, enc[layer], preferred_element_type=jnp.float32) + bias
        return (jnp.maximum(before, 0.0) * live).astype(jnp.bfloat16)

    mine = lax.dynamic_slice_in_dim(resid_in, segment_index * half, half, 0)
    by_dp = spread(mine, "dp").reshape(dps, latents, pair, own_cols)
    by_row = by_dp.transpose(1, 0, 2, 3).reshape(rows, own_cols)
    resid0 = spread(by_row, "latent").transpose(1, 0, 2).reshape(rows, cols)

    active0 = encode(normalize(resid0, small[0][:cols]), 0)
    partial0 = jnp.dot(active0, dec[0], preferred_element_type=jnp.float32).astype(jnp.bfloat16)
    share0 = summed(exchanged(partial0.reshape(latents, dps * pair, cols), "latent"))
    recon0 = summed(exchanged(share0.reshape(dps, pair, cols), "dp"))
    first_row = (lax.axis_index("latent") * dps + lax.axis_index("dp")) * pair
    own_resid0 = lax.dynamic_slice_in_dim(resid0, first_row, pair, 0)
    resid1 = (own_resid0.astype(jnp.float32) + recon0.astype(jnp.float32)).astype(jnp.bfloat16)
    normed1_own = normalize(resid1, small[1][:cols])
    normed1_some = spread(normed1_own, "dp").reshape(dps * pair, cols)
    normed1 = spread(normed1_some, "latent").reshape(rows, cols)

    active1 = encode(normed1, 1)
    partial1 = (
        jnp.dot(active1, dec[1], preferred_element_type=jnp.float32)
        + jnp.dot(active0, dec_cross, preferred_element_type=jnp.float32)
    ).astype(jnp.bfloat16)
    outgoing = jnp.concatenate([partial1, recon0], axis=0)
    outgoing = outgoing.reshape(rows + pair, latents, own_cols).transpose(1, 0, 2)
    incoming = exchanged(outgoing, "latent")
    share1 = summed(incoming[:, :rows]).reshape(latents, dps, pair, own_cols)
    share1 = share1.transpose(1, 0, 2, 3).reshape(dps, latents * pair, own_cols)
    recon1 = summed(exchanged(share1, "dp")).reshape(half, own_rows, own_cols)
    recon0_mine = incoming[:, rows:].reshape(half, own_rows, own_cols)
    other = swapped(jnp.where(is_first, recon1, recon0_mine))
    first = jnp.where(is_first, recon0_mine, other)
    second = jnp.where(is_first, other, recon1)
    return jnp.concatenate([first, second], axis=0)[None]


def solution(mesh):
    return jax.shard_map(
        body,
        mesh=mesh,
        in_specs=(
            P(None, "dp", "latent"),
            P("segment", None),
            P("segment", None, ("latent", "dp")),
            P("segment", ("latent", "dp")),
            P("segment", ("latent", "dp"), None),
            P(("latent", "dp"), None),
            P("segment", None, None, ("latent", "dp"), None),
            P("segment", None, None, ("latent", "dp")),
        ),
        out_specs=P("segment", None, "dp", "latent"),
        check_vma=False,
    )
```

```python
import functools

import jax
import jax.numpy as jnp
from jax import lax
from jax.experimental import pallas as pl
from jax.experimental.pallas import tpu as pltpu
from jax.sharding import PartitionSpec as P

BLK_DEV = 8
BLOCK = 64
PIECES = 4

norm_eps = 1e-06

f32 = jnp.float32
bf16 = jnp.bfloat16


def swapped(value):
    return lax.ppermute(value, "segment", [(0, 1), (1, 0)])


def exchanged(value, axis):
    return lax.all_to_all(value, axis, 0, 0)


def spread(value, axis):
    count = lax.axis_size(axis)
    return exchanged(jnp.broadcast_to(value[None], (count,) + value.shape), axis)


def one_hot(shape, column_of_row):
    row = lax.broadcasted_iota(jnp.int32, shape, 0)
    column = lax.broadcasted_iota(jnp.int32, shape, 1)
    return (column == column_of_row(row)).astype(f32).astype(bf16)


def dot(left, right):
    return jnp.dot(left, right, preferred_element_type=f32)


def copies(source, target, sems, axis):
    size = target.shape[axis] // PIECES
    made = []
    for piece in range(PIECES):
        part = pl.ds(piece * size, size)
        index = (part, slice(None)) if axis == 0 else (slice(None), part)
        made.append(pltpu.make_async_copy(source.at[index], target.at[index], sems.at[piece]))
    return made


def start_from(choose_first, first, second, target, sems, axis):
    @pl.when(choose_first)
    def _():
        for copy in copies(first, target, sems, axis):
            copy.start()

    @pl.when(jnp.logical_not(choose_first))
    def _():
        for copy in copies(second, target, sems, axis):
            copy.start()

    return copies(first, target, sems, axis)


def first_layer(dps, pair, x_ref, gain_ref, bias_ref, live_ref, enc_own, enc_other, dec_own, dec_other,
                part_ref, active_ref, held_ref, enc, dec, enc_sems, dec_sems):
    latents, rows, own_cols = x_ref.shape
    cols = latents * own_cols
    group = rows // dps
    is_first = lax.axis_index("segment") == 0
    latent = lax.axis_index("latent")
    enc_copies = start_from(is_first, enc_own, enc_other, enc, enc_sems, 0)
    dec_copies = start_from(is_first, dec_own, dec_other, dec, dec_sems, 1)

    squares = jnp.zeros((rows, own_cols), f32)
    for piece in range(latents):
        values = x_ref[piece].astype(f32)
        squares += values * values
    scaling = lax.rsqrt(jnp.sum(squares, axis=1, keepdims=True) / cols + norm_eps)

    choose_own = one_hot(
        (dps * pair, rows), lambda row: (row // pair) * group + latent * pair + row % pair
    )
    total = jnp.zeros((rows, enc.shape[1]), f32)
    for piece in range(latents):
        if piece % (latents // PIECES) == 0:
            enc_copies[piece // (latents // PIECES)].wait()
        held_ref[piece] = dot(choose_own, x_ref[piece]).astype(bf16)
        normed = (x_ref[piece].astype(f32) * scaling * gain_ref[pl.ds(piece, 1), :]).astype(bf16)
        total += dot(normed, enc[pl.ds(piece * own_cols, own_cols), :])
    active = (jnp.maximum(total + bias_ref[...], 0.0) * live_ref[...].astype(f32)).astype(bf16)
    active_ref[...] = active
    to_owner = one_hot(
        (rows, rows),
        lambda row: ((row // pair) % dps) * group + row // (dps * pair) * pair + row % pair,
    )
    sorted_active = dot(to_owner, active).astype(bf16)
    size = cols // PIECES
    for piece in range(PIECES):
        dec_copies[piece].wait()
        part = pl.ds(piece * size, size)
        share = dot(sorted_active, dec[:, part]).astype(bf16)
        part_ref[:, :, part] = share.reshape(latents, rows // latents, size)


def second_layer(dps, pair, x_ref, active_ref, bias_ref, live_ref, recon_ref, enc_own, enc_other, dec_own, dec_other,
                 cross_hbm, out_ref, enc, dec, cross, enc_sems, dec_sems, cross_sems):
    latents = x_ref.shape[0]
    cols = x_ref.shape[2]
    rows = active_ref.shape[0]
    group = rows // dps
    own_cols = cols // latents
    is_first = lax.axis_index("segment") == 0
    enc_copies = start_from(is_first, enc_other, enc_own, enc, enc_sems, 0)
    dec_copies = start_from(is_first, dec_other, dec_own, dec, dec_sems, 1)
    cross_copies = copies(cross_hbm, cross, cross_sems, 1)
    for copy in cross_copies:
        copy.start()

    size = cols // PIECES
    total = jnp.zeros((rows, enc.shape[1]), f32)
    for piece in range(PIECES):
        enc_copies[piece].wait()
        part = pl.ds(piece * size, size)
        total += dot(x_ref[:, :, part].reshape(rows, size), enc[part, :])
    active = (jnp.maximum(total + bias_ref[...], 0.0) * live_ref[...].astype(f32)).astype(bf16)
    to_natural = one_hot(
        (rows, rows),
        lambda row: (row % group) // pair * (dps * pair) + row // group * pair + row % pair,
    )
    sorted_active = dot(to_natural, active).astype(bf16)
    earlier = active_ref[...]
    per_piece = latents // PIECES
    for piece in range(PIECES):
        dec_copies[piece].wait()
        cross_copies[piece].wait()
        part = pl.ds(piece * size, size)
        share = dot(sorted_active, dec[:, part]) + dot(earlier, cross[:, part])
        recon = recon_ref[:, part].astype(f32)
        for inner in range(per_piece):
            where = slice(inner * own_cols, (inner + 1) * own_cols)
            out_ref[piece * per_piece + inner, pl.ds(0, rows), :] = share[:, where].astype(bf16)
            out_ref[piece * per_piece + inner, pl.ds(rows, dps * pair), :] = recon[:, where].astype(bf16)


def sum_parts(x_ref, out_ref):
    total = x_ref[0].astype(f32)
    for source in range(1, x_ref.shape[0]):
        total += x_ref[source].astype(f32)
    _, height, width = out_ref.shape
    per_row = total.shape[1] // width
    for piece in range(out_ref.shape[0]):
        down, across = divmod(piece, per_row)
        out_ref[piece] = total[down * height : (down + 1) * height, across * width : (across + 1) * width]


def sum_and_spread(x_ref, out_ref):
    total = x_ref[0]
    for source in range(1, x_ref.shape[0]):
        total += x_ref[source]
    rounded = total.astype(bf16).astype(f32)
    for piece in range(out_ref.shape[0]):
        out_ref[piece] = rounded


def add_and_normalize(pieces_ref, held_ref, gain_ref, out_ref, recon_ref, wide):
    count, height, width = pieces_ref.shape
    cols = wide.shape[1]
    per_row = cols // width
    for piece in range(count):
        down, across = divmod(piece, per_row)
        wide[pl.ds(down * height, height), pl.ds(across * width, width)] = pieces_ref[piece]
    recon = wide[...]
    recon_ref[...] = recon.astype(bf16)
    resid = (held_ref[...].astype(f32) + recon).astype(bf16).astype(f32)
    scaling = lax.rsqrt(jnp.mean(resid * resid, axis=1, keepdims=True) + norm_eps)
    normed = (resid * scaling * gain_ref[...]).astype(bf16)
    for piece in range(out_ref.shape[0]):
        out_ref[piece] = normed


def sum_for_dp(rows, dps, pair, x_ref, out_ref):
    latents, taken, own_cols = x_ref.shape
    total = x_ref[0, pl.ds(0, rows), :].astype(f32)
    for source in range(1, latents):
        total += x_ref[source, pl.ds(0, rows), :].astype(f32)
    out_ref[1] = total.astype(bf16).reshape(dps, rows // dps, own_cols)
    extra = taken - rows
    dp = lax.axis_index("dp")
    choose_own = one_hot(
        (latents * pair, latents * extra),
        lambda row: (row // pair) * extra + dp * pair + row % pair,
    )
    recon = x_ref[:, pl.ds(rows, extra), :].reshape(latents * extra, own_cols)
    recon = dot(choose_own, recon).astype(bf16)
    for piece in range(dps):
        out_ref[0, piece] = recon


def finish(x_ref, out_ref):
    halves, dps = x_ref.shape[:2]
    is_first = lax.axis_index("segment") == 0
    dp = lax.axis_index("dp")
    for half in range(halves):
        total = x_ref[half, 0].astype(f32)
        for source in range(1, dps):
            total += x_ref[half, source].astype(f32)
        kept = x_ref[half, dp].astype(f32)
        out_ref[half] = jnp.where(is_first, kept, total).astype(bf16)


def call(kernel, outs, ins, hbm=0, scratch=(), limit=None):
    vmem = pl.BlockSpec(memory_space=pltpu.VMEM)
    single = not isinstance(outs, (list, tuple))
    return pl.pallas_call(
        kernel,
        out_shape=outs,
        in_specs=[vmem] * (len(ins) - hbm) + [pl.BlockSpec(memory_space=pl.ANY)] * hbm,
        out_specs=vmem if single else [vmem] * len(outs),
        scratch_shapes=list(scratch),
        compiler_params=pltpu.CompilerParams(vmem_limit_bytes=limit),
    )(*ins)


def array(shape, dtype=bf16):
    return jax.ShapeDtypeStruct(shape, dtype)


def body(resid_in, norm_gain, enc_weight, enc_bias, dec_self, dec_cross, block_ids, block_counts):
    segment_index = lax.axis_index("segment")
    is_first = segment_index == 0
    latents = lax.axis_size("latent")
    dps = lax.axis_size("dp")
    batches, own_rows, own_cols = resid_in.shape
    half = batches // 2
    cols = latents * own_cols
    width = enc_weight.shape[2]
    group = half * own_rows
    pair = group // latents
    some = dps * pair
    rows = group * dps

    list_ids = block_ids[0, :, :, 0, :]
    counts = block_counts[0, :, :, 0]
    slot_live = jnp.arange(list_ids.shape[-1], dtype=jnp.int32) < counts[..., None]
    matches = (list_ids[..., None] == jnp.arange(BLK_DEV, dtype=jnp.int32)) & slot_live[..., None]
    live_own = jnp.any(matches, axis=2).astype(f32)
    tiles = live_own.shape[1]

    enc_own, dec_own = enc_weight[0], dec_self[0]
    small_own = jnp.concatenate([norm_gain[0], enc_bias[0], live_own.reshape(-1)])
    enc_other = swapped(enc_own)
    dec_other = swapped(dec_own)
    small_other = swapped(small_own)

    def parts_of(values):
        gain = values[:cols]
        bias = values[cols : cols + width].reshape(1, width)
        live = values[cols + width :].reshape(batches, tiles, BLK_DEV)
        live = lax.dynamic_slice_in_dim(live, segment_index * half, half, 0)
        return gain, bias, jnp.repeat(live.astype(bf16), BLOCK, axis=2)

    gain0, bias0, live0 = parts_of(jnp.where(is_first, small_own, small_other))
    gain1, bias1, live1 = parts_of(jnp.where(is_first, small_other, small_own))
    live0 = jnp.broadcast_to(
        live0.transpose(1, 0, 2)[:, None, :, None, :], (tiles, dps // tiles, half, own_rows, width)
    ).reshape(rows, width)
    live1 = jnp.broadcast_to(
        live1[:, None, :, None, :], (half, latents // half, tiles, some // tiles, width)
    ).reshape(rows, width)

    mine = lax.dynamic_slice_in_dim(resid_in, segment_index * half, half, 0)
    by_dp = spread(mine.reshape(group, own_cols), "dp").reshape(rows, own_cols)
    resid0 = spread(by_dp, "latent")

    weights = [enc_own, enc_other, dec_own, dec_other]
    sems = pltpu.SemaphoreType.DMA((PIECES,))
    partial0, active0, held = call(
        functools.partial(first_layer, dps, pair),
        [array((latents, some, cols)), array((rows, width)), array((latents, some, own_cols))],
        [resid0, gain0.reshape(latents, own_cols), bias0, live0] + weights,
        hbm=4,
        scratch=[pltpu.VMEM(enc_own.shape, bf16), pltpu.VMEM(dec_own.shape, bf16), sems, sems],
        limit=32 * 1024 * 1024,
    )
    held = held.transpose(1, 0, 2).reshape(some, cols)
    down = 2
    block = (dps, some // down, cols * down // dps)
    share0 = call(sum_parts, array(block, f32), [exchanged(partial0, "latent")], limit=16 * 1024 * 1024)
    recon0 = call(sum_and_spread, array(block, f32), [exchanged(share0, "dp")])
    normed1, recon0 = call(
        add_and_normalize,
        [array((latents, some, cols)), array((some, cols))],
        [exchanged(recon0, "dp"), held, gain1.reshape(1, cols)],
        scratch=[pltpu.VMEM((some, cols), f32)],
        limit=16 * 1024 * 1024,
    )
    normed1 = exchanged(normed1, "latent")

    outgoing = call(
        functools.partial(second_layer, dps, pair),
        array((latents, rows + some, own_cols)),
        [normed1, active0, bias1, live1, recon0] + weights + [dec_cross],
        hbm=5,
        scratch=[pltpu.VMEM(enc_own.shape, bf16)] + [pltpu.VMEM(dec_own.shape, bf16)] * 2 + [sems] * 3,
        limit=40 * 1024 * 1024,
    )
    incoming = exchanged(outgoing, "latent")
    share1 = call(
        functools.partial(sum_for_dp, rows, dps, pair),
        array((2, dps, group, own_cols)),
        [incoming],
        limit=16 * 1024 * 1024,
    )
    final = exchanged(share1.reshape(2 * dps, group, own_cols), ("segment", "dp"))
    result = call(finish, array((2, group, own_cols)), [final.reshape(2, dps, group, own_cols)])
    return result.reshape(1, batches, own_rows, own_cols)


def solution(mesh):
    return jax.shard_map(
        body,
        mesh=mesh,
        in_specs=(
            P(None, "dp", "latent"),
            P("segment", None),
            P("segment", None, ("latent", "dp")),
            P("segment", ("latent", "dp")),
            P("segment", ("latent", "dp"), None),
            P(("latent", "dp"), None),
            P("segment", None, None, ("latent", "dp"), None),
            P("segment", None, None, ("latent", "dp")),
        ),
        out_specs=P("segment", None, "dp", "latent"),
        check_vma=False,
    )
```

```python
import functools

import jax
import jax.numpy as jnp
from jax import lax
from jax.experimental import pallas as pl
from jax.experimental.pallas import tpu as pltpu
from jax.sharding import PartitionSpec as P

BLK_DEV = 8
BLOCK = 64
PIECES = 4

norm_eps = 1e-06

f32 = jnp.float32
bf16 = jnp.bfloat16


def swapped(value):
    return lax.ppermute(value, "segment", [(0, 1), (1, 0)])


def exchanged(value, axis):
    return lax.all_to_all(value, axis, 0, 0)


def one_hot(shape, column_of_row):
    row = lax.broadcasted_iota(jnp.int32, shape, 0)
    column = lax.broadcasted_iota(jnp.int32, shape, 1)
    return (column == column_of_row(row)).astype(f32).astype(bf16)


def dot(left, right):
    return jnp.dot(left, right, preferred_element_type=f32)


def copies(source, target, sems, axis):
    size = target.shape[axis] // PIECES
    made = []
    for piece in range(PIECES):
        part = pl.ds(piece * size, size)
        index = (part, slice(None)) if axis == 0 else (slice(None), part)
        made.append(pltpu.make_async_copy(source.at[index], target.at[index], sems.at[piece]))
    return made


def start_from(choose_first, first, second, target, sems, axis):
    @pl.when(choose_first)
    def _():
        for copy in copies(first, target, sems, axis):
            copy.start()

    @pl.when(jnp.logical_not(choose_first))
    def _():
        for copy in copies(second, target, sems, axis):
            copy.start()

    return copies(first, target, sems, axis)


def live_row(list_ref, batch, tile, width):
    block = lax.broadcasted_iota(jnp.int32, (1, width), 1) // BLOCK
    live = jnp.zeros((1, width), f32)
    for slot in range(list_ref.shape[4]):
        live = jnp.where(block == list_ref[0, batch, tile, 0, slot], 1.0, live)
    return live


def live_rows(choose_first, first, second, batch, tile, count, width):
    row = jnp.where(
        choose_first, live_row(first, batch, tile, width), live_row(second, batch, tile, width)
    )
    return jnp.broadcast_to(row, (count, width))


def first_layer(latents, dps, x_ref, gain_own, gain_other, bias_own, bias_other, list_own, list_other,
                enc_own, enc_other, dec_own, dec_other,
                part_hbm, active_ref, held_ref, enc, dec, share, enc_sems, dec_sems, share_sems):
    group = x_ref.shape[1]
    rows = dps * group
    pair = group // latents
    cols = gain_own.shape[1]
    own_cols = cols // latents
    width = enc.shape[1]
    half, tiles = list_own.shape[1] // 2, list_own.shape[2]
    segment = lax.axis_index("segment")
    is_first = segment == 0
    latent = lax.axis_index("latent")
    enc_copies = start_from(is_first, enc_own, enc_other, enc, enc_sems, 0)
    gain = jnp.where(is_first, gain_own[...], gain_other[...])
    bias = jnp.where(is_first, bias_own[...], bias_other[...])
    step_latent = jnp.where(is_first, dps, 1)
    step_dp = jnp.where(is_first, 1, latents)

    def block(piece):
        parts = [x_ref[piece * step_latent + dp * step_dp] for dp in range(dps)]
        return jnp.concatenate(parts, axis=0)[:, :own_cols]

    squares = jnp.zeros((rows, own_cols), f32)
    for piece in range(latents):
        values = block(piece).astype(f32)
        squares += values * values
    scaling = lax.rsqrt(jnp.sum(squares, axis=1, keepdims=True) / cols + norm_eps)

    choose_own = one_hot(
        (dps * pair, rows), lambda row: (row // pair) * group + latent * pair + row % pair
    )
    total = jnp.zeros((rows, width), f32)
    dec_copies = []
    for piece in range(latents):
        if piece % (latents // PIECES) == 0:
            enc_copies[piece // (latents // PIECES)].wait()
            if piece == 0:
                dec_copies = start_from(is_first, dec_own, dec_other, dec, dec_sems, 1)
        own_gain = gain[:, piece * own_cols : (piece + 1) * own_cols]
        values = block(piece)
        held_ref[piece] = dot(choose_own, values).astype(bf16)
        normed = (values.astype(f32) * scaling * own_gain).astype(bf16)
        total += dot(normed, enc[pl.ds(piece * own_cols, own_cols), :])
    live = []
    for tile in range(tiles):
        some = [
            live_rows(is_first, list_own, list_other, segment * half + batch, tile, group // half, width)
            for batch in range(half)
        ]
        live += some * (dps // tiles)
    active = (jnp.maximum(total + bias, 0.0) * jnp.concatenate(live, axis=0)).astype(bf16)
    active_ref[...] = active
    to_owner = one_hot(
        (rows, rows),
        lambda row: ((row // pair) % dps) * group + row // (dps * pair) * pair + row % pair,
    )
    sorted_active = dot(to_owner, active).astype(bf16)
    size = cols // PIECES
    share_copies = []
    for piece in range(PIECES):
        dec_copies[piece].wait()
        part = pl.ds(piece * size, size)
        share[:, :, part] = dot(sorted_active, dec[:, part]).astype(bf16).reshape(latents, rows // latents, size)
        where = (slice(None), slice(None), part)
        copy = pltpu.make_async_copy(share.at[where], part_hbm.at[where], share_sems.at[piece])
        copy.start()
        share_copies.append(copy)
    for copy in share_copies:
        copy.wait()


def cut_decoder(own_segment, *refs):
    *_, dec_hbm, dec_out, dec, dec_part, dec_sems, out_sem = refs
    latents, _, own_cols = dec_out.shape
    size = dec.shape[1] // PIECES
    per_piece = latents // PIECES

    @pl.when(lax.axis_index("segment") == own_segment)
    def _():
        dec_copies = copies(dec_hbm, dec, dec_sems, 1)
        for copy in dec_copies:
            copy.start()
        for piece in range(PIECES):
            dec_copies[piece].wait()
            decoder = dec[:, pl.ds(piece * size, size)].astype(f32)
            for inner in range(per_piece):
                where = slice(inner * own_cols, (inner + 1) * own_cols)
                dec_part[piece * per_piece + inner] = decoder[:, where].astype(bf16)
        copy = pltpu.make_async_copy(dec_part, dec_out, out_sem)
        copy.start()
        copy.wait()


def cross_share(active_ref, cross_hbm, cross_out, cross, cross_part, cross_sems, out_sem):
    latents, _, own_cols = cross_out.shape
    cross_copies = copies(cross_hbm, cross, cross_sems, 1)
    for copy in cross_copies:
        copy.start()
    size = cross.shape[1] // PIECES
    per_piece = latents // PIECES
    earlier = active_ref[...]
    for piece in range(PIECES):
        cross_copies[piece].wait()
        share = dot(earlier, cross[:, pl.ds(piece * size, size)])
        for inner in range(per_piece):
            where = slice(inner * own_cols, (inner + 1) * own_cols)
            cross_part[piece * per_piece + inner] = share[:, where]
    copy = pltpu.make_async_copy(cross_part, cross_out, out_sem)
    copy.start()
    copy.wait()


def second_layer(dps, x_ref, recon_ref, bias_own, bias_other, list_own, list_other,
                 enc_own, enc_other, dec_hbm, cross_hbm, out_ref, enc, dec, cross, enc_sems, dec_sems, cross_sems):
    latents, some, cols = x_ref.shape
    rows = cross.shape[1]
    pair = some // dps
    group = rows // dps
    width = enc.shape[1]
    enc_copies = start_from(lax.axis_index("segment") == 0, enc_other, enc_own, enc, enc_sems, 0)
    dec_copies = copies(dec_hbm, dec, dec_sems, 0)
    cross_copies = copies(cross_hbm, cross, cross_sems, 0)
    half, tiles = list_own.shape[1] // 2, list_own.shape[2]
    segment = lax.axis_index("segment")
    is_first = segment == 0
    bias = jnp.where(is_first, bias_other[...], bias_own[...])
    size = cols // PIECES
    total = jnp.zeros((rows, width), f32)
    for piece in range(PIECES):
        enc_copies[piece].wait()
        dec_copies[piece].start()
        cross_copies[piece].start()
        part = pl.ds(piece * size, size)
        total += dot(x_ref[:, :, part].reshape(rows, size), enc[part, :])
    live = []
    for batch in range(half):
        both = [
            live_rows(is_first, list_other, list_own, segment * half + batch, tile, some // tiles, width)
            for tile in range(tiles)
        ]
        live += both * (latents // half)
    active = (jnp.maximum(total + bias, 0.0) * jnp.concatenate(live, axis=0)).astype(bf16)
    to_natural = one_hot(
        (rows, rows),
        lambda row: (row % group) // pair * some + row // group * pair + row % pair,
    )
    sorted_active = dot(to_natural, active).astype(bf16)
    for piece in range(latents):
        if piece % (latents // PIECES) == 0:
            dec_copies[piece // (latents // PIECES)].wait()
            cross_copies[piece // (latents // PIECES)].wait()
        out_ref[piece, pl.ds(0, rows), :] = (dot(sorted_active, dec[piece]) + cross[piece]).astype(bf16)
        out_ref[piece, pl.ds(rows, some), :] = recon_ref[piece]


def take_own(x_ref, out_ref):
    count, group, padded = out_ref.shape
    half = x_ref.shape[0] // 2
    own_cols = x_ref.shape[2]
    segment = lax.axis_index("segment")
    for batch in range(half):
        mine = x_ref[segment * half + batch].astype(f32)
        mine = jnp.concatenate([mine, jnp.zeros((mine.shape[0], padded - own_cols), f32)], axis=1).astype(bf16)
        for piece in range(count):
            out_ref[piece, pl.ds(batch * mine.shape[0], mine.shape[0]), :] = mine


def repeat(x_ref, out_ref):
    for piece in range(out_ref.shape[0]):
        out_ref[piece] = x_ref[...]


def sum_parts(x_ref, out_ref):
    total = x_ref[0].astype(f32)
    for source in range(1, x_ref.shape[0]):
        total += x_ref[source].astype(f32)
    _, height, width = out_ref.shape
    per_row = total.shape[1] // width
    for piece in range(out_ref.shape[0]):
        down, across = divmod(piece, per_row)
        out_ref[piece] = total[down * height : (down + 1) * height, across * width : (across + 1) * width]


def sum_and_spread(x_ref, out_ref):
    total = x_ref[0]
    for source in range(1, x_ref.shape[0]):
        total += x_ref[source]
    rounded = total.astype(bf16).astype(f32)
    for piece in range(out_ref.shape[0]):
        out_ref[piece] = rounded


def add_and_normalize(pieces_ref, held_ref, gain_own, gain_other, out_ref, recon_ref, wide):
    count, height, width = pieces_ref.shape
    cols = wide.shape[1]
    per_row = cols // width
    for piece in range(count):
        down, across = divmod(piece, per_row)
        wide[pl.ds(down * height, height), pl.ds(across * width, width)] = pieces_ref[piece]
    recon = wide[...]
    own_cols = recon_ref.shape[2]
    for piece in range(recon_ref.shape[0]):
        recon_ref[piece] = recon[:, piece * own_cols : (piece + 1) * own_cols].astype(bf16)
    resid = (held_ref[...].astype(f32) + recon).astype(bf16).astype(f32)
    scaling = lax.rsqrt(jnp.mean(resid * resid, axis=1, keepdims=True) + norm_eps)
    gain = jnp.where(lax.axis_index("segment") == 0, gain_other[...], gain_own[...])
    normed = (resid * scaling * gain).astype(bf16)
    for piece in range(out_ref.shape[0]):
        out_ref[piece] = normed


def sum_for_dp(rows, dps, pair, x_ref, out_ref):
    latents, taken, own_cols = x_ref.shape
    total = x_ref[0, pl.ds(0, rows), :].astype(f32)
    for source in range(1, latents):
        total += x_ref[source, pl.ds(0, rows), :].astype(f32)
    out_ref[1] = total.astype(bf16).reshape(dps, rows // dps, own_cols)
    extra = taken - rows
    dp = lax.axis_index("dp")
    choose_own = one_hot(
        (latents * pair, latents * extra),
        lambda row: (row // pair) * extra + dp * pair + row % pair,
    )
    recon = x_ref[:, pl.ds(rows, extra), :].reshape(latents * extra, own_cols)
    recon = dot(choose_own, recon).astype(bf16)
    for piece in range(dps):
        out_ref[0, piece] = recon


def finish(x_ref, out_ref):
    halves, dps = x_ref.shape[:2]
    is_first = lax.axis_index("segment") == 0
    dp = lax.axis_index("dp")
    for half in range(halves):
        total = x_ref[half, 0].astype(f32)
        for source in range(1, dps):
            total += x_ref[half, source].astype(f32)
        kept = x_ref[half, dp].astype(f32)
        out_ref[half] = jnp.where(is_first, kept, total).astype(bf16)


def call(kernel, outs, ins, scalars=0, hbm=0, scratch=(), limit=16, hbm_outs=0, aliases=None):
    vmem, far = pl.BlockSpec(memory_space=pltpu.VMEM), pl.BlockSpec(memory_space=pltpu.HBM)
    single = not isinstance(outs, (list, tuple))
    specs = [vmem] * (len(ins) - scalars - hbm)
    specs += [pl.BlockSpec(memory_space=pltpu.SMEM)] * scalars
    specs += [far] * hbm
    return pl.pallas_call(
        kernel,
        out_shape=outs,
        in_specs=specs,
        out_specs=vmem if single else [far] * hbm_outs + [vmem] * (len(outs) - hbm_outs),
        scratch_shapes=list(scratch),
        input_output_aliases=aliases or {},
        compiler_params=pltpu.CompilerParams(vmem_limit_bytes=limit * 1024 * 1024),
    )(*[placed(value, index, len(ins), hbm) for index, value in enumerate(ins)])


def placed(value, index, count, hbm):
    return pltpu.with_memory_space_constraint(value, pltpu.HBM) if index >= count - hbm else value


def array(shape, dtype=bf16, space=None):
    return jax.ShapeDtypeStruct(shape, dtype) if space is None else space(shape, dtype)


def body(resid_in, norm_gain, enc_weight, enc_bias, dec_self, dec_cross, block_ids, block_counts):
    is_first = lax.axis_index("segment") == 0
    latents = lax.axis_size("latent")
    dps = lax.axis_size("dp")
    batches, own_rows, own_cols = resid_in.shape
    cols = latents * own_cols
    width = enc_weight.shape[2]
    group = batches // 2 * own_rows
    some = dps * group // latents
    rows = group * dps
    padded = own_cols + -own_cols % 128

    enc_own, dec_own = enc_weight[0], dec_self[0]
    weights = [enc_own, swapped(enc_own), dec_own, swapped(dec_own)]
    gains = [norm_gain, swapped(norm_gain)]
    biases = [enc_bias, swapped(enc_bias)]
    slot = lax.broadcasted_iota(jnp.int32, block_ids.shape, block_ids.ndim - 1)
    listed = jnp.where(slot < block_counts[..., None], block_ids, -1)
    lists = [listed, swapped(listed)]

    def dp_first(resid):
        mine = call(take_own, array((dps, group, padded)), [resid])
        some_rows = exchanged(mine, "dp").reshape(rows, padded)
        every = call(repeat, array((latents, rows, padded)), [some_rows])
        return exchanged(every, "latent").reshape(latents * dps, group, padded)

    def latent_first(resid):
        mine = call(take_own, array((latents, group, padded)), [resid])
        some_cols = exchanged(mine, "latent").reshape(latents * group, padded)
        every = call(repeat, array((dps, latents * group, padded)), [some_cols])
        return exchanged(every, "dp").reshape(latents * dps, group, padded)

    resid0 = lax.cond(is_first, dp_first, latent_first, resid_in)

    sems = pltpu.SemaphoreType.DMA((PIECES,))
    enc_space, dec_space = pltpu.VMEM(enc_own.shape, bf16), pltpu.VMEM(dec_own.shape, bf16)
    partial0, active0, held = call(
        functools.partial(first_layer, latents, dps),
        [array((latents, some, cols), space=pltpu.HBM), array((rows, width)), array((latents, some, own_cols))],
        [resid0] + gains + biases + lists + weights,
        scalars=2,
        hbm=4,
        scratch=[enc_space, dec_space, pltpu.VMEM((latents, some, cols), bf16)] + [sems] * 3,
        limit=26,
        hbm_outs=1,
    )
    held = held.transpose(1, 0, 2).reshape(some, cols)
    dec_parts = pltpu.VMEM((latents, width, own_cols), bf16)
    cross_parts = pltpu.VMEM((latents, rows, own_cols), f32)
    one_sem = pltpu.SemaphoreType.DMA(())
    dec_cut = array((latents, width, own_cols), space=pltpu.HBM)
    cut_space = dict(scratch=[dec_space, dec_parts, sems, one_sem], limit=24, hbm_outs=1)
    dec1 = call(functools.partial(cut_decoder, 1), [dec_cut], [dec_own], hbm=1, **cut_space)[0]
    partial0, dec1 = lax.optimization_barrier((partial0, dec1))
    dec1 = call(
        functools.partial(cut_decoder, 0), [dec_cut], [dec1, weights[3]], hbm=2, aliases={0: 0}, **cut_space
    )[0]
    cross0 = call(
        cross_share,
        [array((latents, rows, own_cols), f32, space=pltpu.HBM)],
        [active0, dec_cross],
        hbm=1,
        scratch=[dec_space, cross_parts, sems, one_sem],
        limit=24,
        hbm_outs=1,
    )[0]
    down = 2
    block = (dps, some // down, cols * down // dps)
    arrived = exchanged(partial0, "latent")
    arrived, held, dec1, cross0 = lax.optimization_barrier((arrived, held, dec1, cross0))
    share0 = call(sum_parts, array(block, f32), [arrived])
    recon0 = call(sum_and_spread, array(block, f32), [exchanged(share0, "dp")])
    normed1, recon0 = call(
        add_and_normalize,
        [array((latents, some, cols)), array((latents, some, own_cols))],
        [exchanged(recon0, "dp"), held] + gains,
        scratch=[pltpu.VMEM((some, cols), f32)],
    )
    normed1 = exchanged(normed1, "latent")

    outgoing = call(
        functools.partial(second_layer, dps),
        array((latents, rows + some, own_cols)),
        [normed1, recon0] + biases + lists + weights[:2] + [dec1, cross0],
        scalars=2,
        hbm=4,
        scratch=[enc_space, dec_parts, cross_parts] + [sems] * 3,
        limit=32,
    )
    incoming = exchanged(outgoing, "latent")
    share1 = call(
        functools.partial(sum_for_dp, rows, dps, some // dps),
        array((2, dps, group, own_cols)),
        [incoming],
    )
    final = exchanged(share1.reshape(2 * dps, group, own_cols), ("segment", "dp"))
    result = call(finish, array((2, group, own_cols)), [final.reshape(2, dps, group, own_cols)])
    return result.reshape(1, batches, own_rows, own_cols)


def solution(mesh):
    return jax.shard_map(
        body,
        mesh=mesh,
        in_specs=(
            P(None, "dp", "latent"),
            P("segment", None),
            P("segment", None, ("latent", "dp")),
            P("segment", ("latent", "dp")),
            P("segment", ("latent", "dp"), None),
            P(("latent", "dp"), None),
            P("segment", None, None, ("latent", "dp"), None),
            P("segment", None, None, ("latent", "dp")),
        ),
        out_specs=P("segment", None, "dp", "latent"),
        check_vma=False,
    )
```

```python
import functools

import jax
import jax.numpy as jnp
from jax import lax
from jax.experimental import pallas as pl
from jax.experimental.pallas import tpu as pltpu
from jax.sharding import PartitionSpec as P

BLK_DEV = 8
BLOCK = 64
PIECES = 4
LANES = 128

norm_eps = 1e-06

f32 = jnp.float32
bf16 = jnp.bfloat16


def swapped(value):
    return lax.ppermute(value, "segment", [(0, 1), (1, 0)])


def exchanged(value, axis):
    return lax.all_to_all(value, axis, 0, 0)


def one_hot(shape, column_of_row):
    row = lax.broadcasted_iota(jnp.int32, shape, 0)
    column = lax.broadcasted_iota(jnp.int32, shape, 1)
    return (column == column_of_row(row)).astype(f32).astype(bf16)


def dot(left, right):
    return jnp.dot(left, right, preferred_element_type=f32)


def copies(source, target, sems, axis):
    size = target.shape[axis] // PIECES
    made = []
    for piece in range(PIECES):
        part = pl.ds(piece * size, size)
        index = (part, slice(None)) if axis == 0 else (slice(None), part)
        made.append(pltpu.make_async_copy(source.at[index], target.at[index], sems.at[piece]))
    return made


def start_from(choose_first, first, second, target, sems, axis):
    @pl.when(choose_first)
    def _():
        for copy in copies(first, target, sems, axis):
            copy.start()

    @pl.when(jnp.logical_not(choose_first))
    def _():
        for copy in copies(second, target, sems, axis):
            copy.start()

    return copies(first, target, sems, axis)


def live_row(list_ref, batch, tile, width):
    block = lax.broadcasted_iota(jnp.int32, (1, width), 1) // BLOCK
    live = jnp.zeros((1, width), f32)
    for slot in range(list_ref.shape[4]):
        live = jnp.where(block == list_ref[0, batch, tile, 0, slot], 1.0, live)
    return live


def live_rows(choose_first, first, second, batch, tile, count, width):
    row = jnp.where(
        choose_first, live_row(first, batch, tile, width), live_row(second, batch, tile, width)
    )
    return jnp.broadcast_to(row, (count, width))


def folded(values):
    quarter = values.shape[0] // 4
    right = values[:, LANES:]
    spare = LANES - right.shape[1]
    last = right[3 * quarter :]
    blocks = [
        jnp.concatenate(
            [right[index * quarter : (index + 1) * quarter], last[:, index * spare : (index + 1) * spare]], axis=1
        )
        for index in range(3)
    ]
    return jnp.concatenate([values[:, :LANES]] + blocks, axis=0)


def right_part(blocks, width):
    quarter = blocks.shape[0] // 3
    last = [blocks[index * quarter : (index + 1) * quarter, width:] for index in range(3)]
    return jnp.concatenate([blocks[:, :width], jnp.concatenate(last, axis=1)], axis=0)


def first_layer(latents, dps, x_ref, gain_own, gain_other, bias_own, bias_other, list_own, list_other,
                enc_own, enc_other, dec_own, dec_other,
                part_hbm, active_ref, held_ref, x, enc, dec, share, enc_sems, dec_sems, share_sems):
    rows = x.shape[1]
    group = rows // dps
    pair = group // latents
    cols = gain_own.shape[1]
    own_cols = cols // latents
    width = enc.shape[1]
    half, tiles = list_own.shape[1] // 2, list_own.shape[2]
    segment = lax.axis_index("segment")
    is_first = segment == 0
    latent = lax.axis_index("latent")
    enc_copies = start_from(is_first, enc_own, enc_other, enc, enc_sems, 0)
    gain = jnp.where(is_first, gain_own[...], gain_other[...])
    bias = jnp.where(is_first, bias_own[...], bias_other[...])
    extra = own_cols - LANES
    shard = x_ref.shape[0] // latents

    @pl.when(is_first)
    def _():
        for piece in range(latents):
            start = piece * shard
            x[piece, :, pl.ds(0, LANES)] = x_ref[pl.ds(start, rows), :]
            right = right_part(x_ref[pl.ds(start + rows, shard - rows), :].astype(f32), extra)
            x[piece, :, pl.ds(LANES, extra)] = right.astype(bf16)

    @pl.when(jnp.logical_not(is_first))
    def _():
        shard = x_ref.shape[0] // dps
        whole = latents * group
        for dp in range(dps):
            start = dp * shard
            right = right_part(x_ref[pl.ds(start + whole, shard - whole), :].astype(f32), extra).astype(bf16)
            for piece in range(latents):
                mine = slice(piece * group, (piece + 1) * group)
                to = pl.ds(dp * group, group)
                x[piece, to, pl.ds(0, LANES)] = x_ref[pl.ds(start + piece * group, group), :]
                x[piece, to, pl.ds(LANES, extra)] = right[mine]

    squares = jnp.zeros((rows, own_cols), f32)
    for piece in range(latents):
        values = x[piece].astype(f32)
        squares += values * values
    scaling = lax.rsqrt(jnp.sum(squares, axis=1, keepdims=True) / cols + norm_eps)

    choose_own = one_hot(
        (dps * pair, rows), lambda row: (row // pair) * group + latent * pair + row % pair
    )
    total = jnp.zeros((rows, width), f32)
    dec_copies = []
    for piece in range(latents):
        if piece % (latents // PIECES) == 0:
            enc_copies[piece // (latents // PIECES)].wait()
            if piece == 0:
                dec_copies = start_from(is_first, dec_own, dec_other, dec, dec_sems, 1)
        own_gain = gain[:, piece * own_cols : (piece + 1) * own_cols]
        values = x[piece]
        held_ref[piece] = dot(choose_own, values).astype(bf16)
        normed = (values.astype(f32) * scaling * own_gain).astype(bf16)
        total += dot(normed, enc[pl.ds(piece * own_cols, own_cols), :])
    live = []
    for tile in range(tiles):
        some = [
            live_rows(is_first, list_own, list_other, segment * half + batch, tile, group // half, width)
            for batch in range(half)
        ]
        live += some * (dps // tiles)
    active = (jnp.maximum(total + bias, 0.0) * jnp.concatenate(live, axis=0)).astype(bf16)
    active_ref[...] = active
    to_owner = one_hot(
        (rows, rows),
        lambda row: ((row // pair) % dps) * group + row // (dps * pair) * pair + row % pair,
    )
    sorted_active = dot(to_owner, active).astype(bf16)
    size = cols // PIECES
    share_copies = []
    for piece in range(PIECES):
        dec_copies[piece].wait()
        part = pl.ds(piece * size, size)
        share[:, :, part] = dot(sorted_active, dec[:, part]).astype(bf16).reshape(latents, rows // latents, size)
        where = (slice(None), slice(None), part)
        copy = pltpu.make_async_copy(share.at[where], part_hbm.at[where], share_sems.at[piece])
        copy.start()
        share_copies.append(copy)
    for copy in share_copies:
        copy.wait()


def cut_decoder(own_segment, *refs):
    *_, dec_hbm, dec_out, dec, dec_part, dec_sems, out_sem = refs
    latents, _, own_cols = dec_out.shape
    size = dec.shape[1] // PIECES
    per_piece = latents // PIECES

    @pl.when(lax.axis_index("segment") == own_segment)
    def _():
        dec_copies = copies(dec_hbm, dec, dec_sems, 1)
        for copy in dec_copies:
            copy.start()
        for piece in range(PIECES):
            dec_copies[piece].wait()
            decoder = dec[:, pl.ds(piece * size, size)].astype(f32)
            for inner in range(per_piece):
                where = slice(inner * own_cols, (inner + 1) * own_cols)
                dec_part[piece * per_piece + inner] = decoder[:, where].astype(bf16)
        copy = pltpu.make_async_copy(dec_part, dec_out, out_sem)
        copy.start()
        copy.wait()


def cross_share(own_segment, *refs):
    active_ref, *_, cross_hbm, cross_out, cross, cross_part, cross_sems, out_sem = refs
    latents, _, own_cols = cross_out.shape
    size = cross.shape[1] // PIECES
    per_piece = latents // PIECES

    @pl.when(lax.axis_index("segment") == own_segment)
    def _():
        cross_copies = copies(cross_hbm, cross, cross_sems, 1)
        for copy in cross_copies:
            copy.start()
        earlier = active_ref[...]
        for piece in range(PIECES):
            cross_copies[piece].wait()
            share = dot(earlier, cross[:, pl.ds(piece * size, size)])
            for inner in range(per_piece):
                where = slice(inner * own_cols, (inner + 1) * own_cols)
                cross_part[piece * per_piece + inner] = share[:, where]
        copy = pltpu.make_async_copy(cross_part, cross_out, out_sem)
        copy.start()
        copy.wait()


def second_layer(dps, x_ref, recon_ref, bias_own, bias_other, list_own, list_other,
                 enc_own, enc_other, dec_hbm, cross_hbm, out_ref, enc, dec, cross, enc_sems, dec_sems, cross_sems):
    latents, some, cols = x_ref.shape
    rows = cross.shape[1]
    pair = some // dps
    group = rows // dps
    width = enc.shape[1]
    enc_copies = start_from(lax.axis_index("segment") == 0, enc_other, enc_own, enc, enc_sems, 0)
    dec_copies = copies(dec_hbm, dec, dec_sems, 0)
    cross_copies = copies(cross_hbm, cross, cross_sems, 0)
    half, tiles = list_own.shape[1] // 2, list_own.shape[2]
    segment = lax.axis_index("segment")
    is_first = segment == 0
    bias = jnp.where(is_first, bias_other[...], bias_own[...])
    size = cols // PIECES
    total = jnp.zeros((rows, width), f32)
    for piece in range(PIECES):
        enc_copies[piece].wait()
        dec_copies[piece].start()
        cross_copies[piece].start()
        part = pl.ds(piece * size, size)
        total += dot(x_ref[:, :, part].reshape(rows, size), enc[part, :])
    live = []
    for batch in range(half):
        both = [
            live_rows(is_first, list_other, list_own, segment * half + batch, tile, some // tiles, width)
            for tile in range(tiles)
        ]
        live += both * (latents // half)
    active = (jnp.maximum(total + bias, 0.0) * jnp.concatenate(live, axis=0)).astype(bf16)
    to_natural = one_hot(
        (rows, rows),
        lambda row: (row % group) // pair * some + row // group * pair + row % pair,
    )
    sorted_active = dot(to_natural, active).astype(bf16)
    for piece in range(latents):
        if piece % (latents // PIECES) == 0:
            dec_copies[piece // (latents // PIECES)].wait()
            cross_copies[piece // (latents // PIECES)].wait()
        share = folded(dot(sorted_active, dec[piece]) + cross[piece]).astype(bf16)
        recon = recon_ref[piece]
        extra = recon.shape[1] - LANES
        filled = share.shape[0]
        out_ref[piece, pl.ds(0, filled), :] = share
        out_ref[piece, pl.ds(filled, some), :] = recon[:, :LANES]
        out_ref[piece, pl.ds(filled + some, some), pl.ds(0, extra)] = recon[:, LANES:]
        out_ref[piece, pl.ds(filled + some, some), pl.ds(extra, LANES - extra)] = jnp.zeros((some, LANES - extra), bf16)


def take_own(x_ref, out_ref):
    count, group, padded = out_ref.shape
    half = x_ref.shape[0] // 2
    own_cols = x_ref.shape[2]
    segment = lax.axis_index("segment")
    for batch in range(half):
        mine = x_ref[segment * half + batch].astype(f32)
        mine = jnp.concatenate([mine, jnp.zeros((mine.shape[0], padded - own_cols), f32)], axis=1).astype(bf16)
        for piece in range(count):
            out_ref[piece, pl.ds(batch * mine.shape[0], mine.shape[0]), :] = mine


def repeat(own_cols, x_ref, out_ref):
    values = folded(x_ref[...].astype(f32)[:, :own_cols]).astype(bf16)
    for piece in range(out_ref.shape[0]):
        out_ref[piece] = values


def sum_parts(x_ref, out_ref):
    total = x_ref[0].astype(f32)
    for source in range(1, x_ref.shape[0]):
        total += x_ref[source].astype(f32)
    _, height, width = out_ref.shape
    per_row = total.shape[1] // width
    for piece in range(out_ref.shape[0]):
        down, across = divmod(piece, per_row)
        out_ref[piece] = total[down * height : (down + 1) * height, across * width : (across + 1) * width]


def sum_and_spread(x_ref, out_ref):
    total = x_ref[0]
    for source in range(1, x_ref.shape[0]):
        total += x_ref[source]
    rounded = total.astype(bf16).astype(f32)
    for piece in range(out_ref.shape[0]):
        out_ref[piece] = rounded


def add_and_normalize(pieces_ref, held_ref, gain_own, gain_other, out_ref, recon_ref, wide):
    count, height, width = pieces_ref.shape
    cols = wide.shape[1]
    per_row = cols // width
    for piece in range(count):
        down, across = divmod(piece, per_row)
        wide[pl.ds(down * height, height), pl.ds(across * width, width)] = pieces_ref[piece]
    recon = wide[...]
    own_cols = recon_ref.shape[2]
    for piece in range(recon_ref.shape[0]):
        recon_ref[piece] = recon[:, piece * own_cols : (piece + 1) * own_cols].astype(bf16)
    resid = (held_ref[...].astype(f32) + recon).astype(bf16).astype(f32)
    scaling = lax.rsqrt(jnp.mean(resid * resid, axis=1, keepdims=True) + norm_eps)
    gain = jnp.where(lax.axis_index("segment") == 0, gain_other[...], gain_own[...])
    normed = (resid * scaling * gain).astype(bf16)
    for piece in range(out_ref.shape[0]):
        out_ref[piece] = normed


def sum_for_dp(rows, dps, pair, x_ref, out_ref):
    latents = x_ref.shape[0]
    some = dps * pair
    filled = x_ref.shape[1] - 2 * some
    own_cols = out_ref.shape[3]
    extra = own_cols - LANES
    total = x_ref[0, pl.ds(0, filled), :].astype(f32)
    for source in range(1, latents):
        total += x_ref[source, pl.ds(0, filled), :].astype(f32)
    total = jnp.concatenate([total[:rows], right_part(total[rows:], extra)], axis=1)
    out_ref[1] = total.astype(bf16).reshape(dps, rows // dps, own_cols)
    dp = lax.axis_index("dp")
    choose_own = one_hot(
        (latents * pair, latents * some),
        lambda row: (row // pair) * some + dp * pair + row % pair,
    )
    left = x_ref[:, pl.ds(filled, some), :].reshape(latents * some, LANES)
    right = x_ref[:, pl.ds(filled + some, some), :].reshape(latents * some, LANES)
    recon = jnp.concatenate([dot(choose_own, left), dot(choose_own, right)[:, :extra]], axis=1).astype(bf16)
    for piece in range(dps):
        out_ref[0, piece] = recon


def finish(x_ref, out_ref):
    halves, dps = x_ref.shape[:2]
    is_first = lax.axis_index("segment") == 0
    dp = lax.axis_index("dp")
    for half in range(halves):
        total = x_ref[half, 0].astype(f32)
        for source in range(1, dps):
            total += x_ref[half, source].astype(f32)
        kept = x_ref[half, dp].astype(f32)
        out_ref[half] = jnp.where(is_first, kept, total).astype(bf16)


def call(kernel, outs, ins, scalars=0, hbm=0, scratch=(), limit=16, hbm_outs=0, aliases=None):
    vmem, far = pl.BlockSpec(memory_space=pltpu.VMEM), pl.BlockSpec(memory_space=pltpu.HBM)
    single = not isinstance(outs, (list, tuple))
    specs = [vmem] * (len(ins) - scalars - hbm)
    specs += [pl.BlockSpec(memory_space=pltpu.SMEM)] * scalars
    specs += [far] * hbm
    return pl.pallas_call(
        kernel,
        out_shape=outs,
        in_specs=specs,
        out_specs=vmem if single else [far] * hbm_outs + [vmem] * (len(outs) - hbm_outs),
        scratch_shapes=list(scratch),
        input_output_aliases=aliases or {},
        compiler_params=pltpu.CompilerParams(vmem_limit_bytes=limit * 1024 * 1024),
    )(*[placed(value, index, len(ins), hbm) for index, value in enumerate(ins)])


def placed(value, index, count, hbm):
    return pltpu.with_memory_space_constraint(value, pltpu.HBM) if index >= count - hbm else value


def array(shape, dtype=bf16, space=None):
    return jax.ShapeDtypeStruct(shape, dtype) if space is None else space(shape, dtype)


def body(resid_in, norm_gain, enc_weight, enc_bias, dec_self, dec_cross, block_ids, block_counts):
    is_first = lax.axis_index("segment") == 0
    latents = lax.axis_size("latent")
    dps = lax.axis_size("dp")
    batches, own_rows, own_cols = resid_in.shape
    cols = latents * own_cols
    width = enc_weight.shape[2]
    group = batches // 2 * own_rows
    some = dps * group // latents
    rows = group * dps
    padded = own_cols + -own_cols % 128

    enc_own, dec_own = enc_weight[0], dec_self[0]
    weights = [enc_own, swapped(enc_own), dec_own, swapped(dec_own)]
    gains = [norm_gain, swapped(norm_gain)]
    biases = [enc_bias, swapped(enc_bias)]
    slot = lax.broadcasted_iota(jnp.int32, block_ids.shape, block_ids.ndim - 1)
    listed = jnp.where(slot < block_counts[..., None], block_ids, -1)
    lists = [listed, swapped(listed)]

    def dp_first(resid):
        mine = call(take_own, array((dps, group, padded)), [resid])
        some_rows = exchanged(mine, "dp").reshape(rows, padded)
        every = call(functools.partial(repeat, own_cols), array((latents, rows * 7 // 4, LANES)), [some_rows])
        return exchanged(every, "latent").reshape(-1, LANES)

    def latent_first(resid):
        mine = call(take_own, array((latents, group, padded)), [resid])
        some_cols = exchanged(mine, "latent").reshape(latents * group, padded)
        every = call(
            functools.partial(repeat, own_cols), array((dps, latents * group * 7 // 4, LANES)), [some_cols]
        )
        return exchanged(every, "dp").reshape(-1, LANES)

    resid0 = lax.cond(is_first, dp_first, latent_first, resid_in)

    sems = pltpu.SemaphoreType.DMA((PIECES,))
    enc_space, dec_space = pltpu.VMEM(enc_own.shape, bf16), pltpu.VMEM(dec_own.shape, bf16)
    partial0, active0, held = call(
        functools.partial(first_layer, latents, dps),
        [array((latents, some, cols), space=pltpu.HBM), array((rows, width)), array((latents, some, own_cols))],
        [resid0] + gains + biases + lists + weights,
        scalars=2,
        hbm=4,
        scratch=[pltpu.VMEM((latents, rows, own_cols), bf16), enc_space, dec_space, pltpu.VMEM((latents, some, cols), bf16)] + [sems] * 3,
        limit=26,
        hbm_outs=1,
    )
    held = held.transpose(1, 0, 2).reshape(some, cols)
    dec_parts = pltpu.VMEM((latents, width, own_cols), bf16)
    cross_parts = pltpu.VMEM((latents, rows, own_cols), f32)
    one_sem = pltpu.SemaphoreType.DMA(())
    dec_cut = array((latents, width, own_cols), space=pltpu.HBM)
    cut_space = dict(scratch=[dec_space, dec_parts, sems, one_sem], limit=24, hbm_outs=1)
    dec1 = call(functools.partial(cut_decoder, 1), [dec_cut], [dec_own], hbm=1, **cut_space)[0]
    cross_cut = array((latents, rows, own_cols), f32, space=pltpu.HBM)
    cross_space = dict(scratch=[dec_space, cross_parts, sems, one_sem], limit=24, hbm_outs=1)
    cross0 = call(functools.partial(cross_share, 1), [cross_cut], [active0, dec_cross], hbm=1, **cross_space)[0]
    partial0, dec1, cross0 = lax.optimization_barrier((partial0, dec1, cross0))
    dec1 = call(
        functools.partial(cut_decoder, 0), [dec_cut], [dec1, weights[3]], hbm=2, aliases={0: 0}, **cut_space
    )[0]
    cross0 = call(
        functools.partial(cross_share, 0), [cross_cut], [active0, cross0, dec_cross], hbm=2, aliases={1: 0}, **cross_space
    )[0]
    down = 2
    block = (dps, some // down, cols * down // dps)
    arrived = exchanged(partial0, "latent")
    arrived, held, dec1, cross0 = lax.optimization_barrier((arrived, held, dec1, cross0))
    share0 = call(sum_parts, array(block, f32), [arrived])
    recon0 = call(sum_and_spread, array(block, f32), [exchanged(share0, "dp")])
    normed1, recon0 = call(
        add_and_normalize,
        [array((latents, some, cols)), array((latents, some, own_cols))],
        [exchanged(recon0, "dp"), held] + gains,
        scratch=[pltpu.VMEM((some, cols), f32)],
    )
    normed1 = exchanged(normed1, "latent")

    outgoing = call(
        functools.partial(second_layer, dps),
        array((latents, rows * 7 // 4 + 2 * some, LANES)),
        [normed1, recon0] + biases + lists + weights[:2] + [dec1, cross0],
        scalars=2,
        hbm=4,
        scratch=[enc_space, dec_parts, cross_parts] + [sems] * 3,
        limit=32,
    )
    incoming = exchanged(outgoing, "latent")
    share1 = call(
        functools.partial(sum_for_dp, rows, dps, some // dps),
        array((2, dps, group, own_cols)),
        [incoming],
    )
    final = exchanged(share1.reshape(2 * dps, group, own_cols), ("segment", "dp"))
    result = call(finish, array((2, group, own_cols)), [final.reshape(2, dps, group, own_cols)])
    return result.reshape(1, batches, own_rows, own_cols)


def solution(mesh):
    return jax.shard_map(
        body,
        mesh=mesh,
        in_specs=(
            P(None, "dp", "latent"),
            P("segment", None),
            P("segment", None, ("latent", "dp")),
            P("segment", ("latent", "dp")),
            P("segment", ("latent", "dp"), None),
            P(("latent", "dp"), None),
            P("segment", None, None, ("latent", "dp"), None),
            P("segment", None, None, ("latent", "dp")),
        ),
        out_specs=P("segment", None, "dp", "latent"),
        check_vma=False,
    )
```

```python
import functools

import jax
import jax.numpy as jnp
from jax import lax
from jax.experimental import pallas as pl
from jax.experimental.pallas import tpu as pltpu
from jax.sharding import PartitionSpec as P

BLK_DEV = 8
BLOCK = 64
PIECES = 4
LANES = 128

norm_eps = 1e-06

f32 = jnp.float32
bf16 = jnp.bfloat16


def swapped(value):
    return lax.ppermute(value, "segment", [(0, 1), (1, 0)])


def exchanged(value, axis):
    return lax.all_to_all(value, axis, 0, 0)


def one_hot(shape, column_of_row):
    row = lax.broadcasted_iota(jnp.int32, shape, 0)
    column = lax.broadcasted_iota(jnp.int32, shape, 1)
    return (column == column_of_row(row)).astype(f32).astype(bf16)


def dot(left, right):
    return jnp.dot(left, right, preferred_element_type=f32)


def copies(source, target, sems, axis):
    size = target.shape[axis] // PIECES
    made = []
    for piece in range(PIECES):
        part = pl.ds(piece * size, size)
        index = (part, slice(None)) if axis == 0 else (slice(None), part)
        made.append(pltpu.make_async_copy(source.at[index], target.at[index], sems.at[piece]))
    return made


def start_from(choose_first, first, second, target, sems, axis):
    @pl.when(choose_first)
    def _():
        for copy in copies(first, target, sems, axis):
            copy.start()

    @pl.when(jnp.logical_not(choose_first))
    def _():
        for copy in copies(second, target, sems, axis):
            copy.start()

    return copies(first, target, sems, axis)


def live_row(list_ref, batch, tile, width):
    block = lax.broadcasted_iota(jnp.int32, (1, width), 1) // BLOCK
    live = jnp.zeros((1, width), f32)
    for slot in range(list_ref.shape[4]):
        live = jnp.where(block == list_ref[0, batch, tile, 0, slot], 1.0, live)
    return live


def live_rows(choose_first, first, second, batch, tile, count, width):
    row = jnp.where(
        choose_first, live_row(first, batch, tile, width), live_row(second, batch, tile, width)
    )
    return jnp.broadcast_to(row, (count, width))


def folded(values):
    quarter = values.shape[0] // 4
    right = values[:, LANES:]
    spare = LANES - right.shape[1]
    last = right[3 * quarter :]
    blocks = [
        jnp.concatenate(
            [right[index * quarter : (index + 1) * quarter], last[:, index * spare : (index + 1) * spare]], axis=1
        )
        for index in range(3)
    ]
    return jnp.concatenate([values[:, :LANES]] + blocks, axis=0)


def right_part(blocks, width):
    quarter = blocks.shape[0] // 3
    last = [blocks[index * quarter : (index + 1) * quarter, width:] for index in range(3)]
    return jnp.concatenate([blocks[:, :width], jnp.concatenate(last, axis=1)], axis=0)


def first_layer(latents, dps, x_ref, gain_own, gain_other, bias_own, bias_other, list_own, list_other,
                enc_own, enc_other, dec_own, dec_other,
                part_hbm, active_ref, held_ref, x, enc, dec, share, enc_sems, dec_sems, share_sems):
    rows = x.shape[1]
    group = rows // dps
    pair = group // latents
    cols = gain_own.shape[1]
    own_cols = cols // latents
    width = enc.shape[1]
    half, tiles = list_own.shape[1] // 2, list_own.shape[2]
    segment = lax.axis_index("segment")
    is_first = segment == 0
    latent = lax.axis_index("latent")
    enc_copies = start_from(is_first, enc_own, enc_other, enc, enc_sems, 0)
    gain = jnp.where(is_first, gain_own[...], gain_other[...])
    bias = jnp.where(is_first, bias_own[...], bias_other[...])
    extra = own_cols - LANES
    shard = x_ref.shape[0] // latents

    @pl.when(is_first)
    def _():
        for piece in range(latents):
            start = piece * shard
            x[piece, :, pl.ds(0, LANES)] = x_ref[pl.ds(start, rows), :]
            right = right_part(x_ref[pl.ds(start + rows, shard - rows), :].astype(f32), extra)
            x[piece, :, pl.ds(LANES, extra)] = right.astype(bf16)

    @pl.when(jnp.logical_not(is_first))
    def _():
        shard = x_ref.shape[0] // dps
        whole = latents * group
        for dp in range(dps):
            start = dp * shard
            right = right_part(x_ref[pl.ds(start + whole, shard - whole), :].astype(f32), extra).astype(bf16)
            for piece in range(latents):
                mine = slice(piece * group, (piece + 1) * group)
                to = pl.ds(dp * group, group)
                x[piece, to, pl.ds(0, LANES)] = x_ref[pl.ds(start + piece * group, group), :]
                x[piece, to, pl.ds(LANES, extra)] = right[mine]

    squares = jnp.zeros((rows, own_cols), f32)
    for piece in range(latents):
        values = x[piece].astype(f32)
        squares += values * values
    scaling = lax.rsqrt(jnp.sum(squares, axis=1, keepdims=True) / cols + norm_eps)

    choose_own = one_hot(
        (dps * pair, rows), lambda row: (row // pair) * group + latent * pair + row % pair
    )
    total = jnp.zeros((rows, width), f32)
    dec_copies = []
    for piece in range(latents):
        if piece % (latents // PIECES) == 0:
            enc_copies[piece // (latents // PIECES)].wait()
            if piece == 0:
                dec_copies = start_from(is_first, dec_own, dec_other, dec, dec_sems, 1)
        own_gain = gain[:, piece * own_cols : (piece + 1) * own_cols]
        values = x[piece]
        held_ref[piece] = dot(choose_own, values).astype(bf16)
        normed = (values.astype(f32) * scaling * own_gain).astype(bf16)
        total += dot(normed, enc[pl.ds(piece * own_cols, own_cols), :])
    live = []
    for tile in range(tiles):
        some = [
            live_rows(is_first, list_own, list_other, segment * half + batch, tile, group // half, width)
            for batch in range(half)
        ]
        live += some * (dps // tiles)
    active = (jnp.maximum(total + bias, 0.0) * jnp.concatenate(live, axis=0)).astype(bf16)
    active_ref[...] = active
    to_owner = one_hot(
        (rows, rows),
        lambda row: ((row // pair) % dps) * group + row // (dps * pair) * pair + row % pair,
    )
    sorted_active = dot(to_owner, active).astype(bf16)
    size = cols // PIECES
    share_copies = []
    for piece in range(PIECES):
        dec_copies[piece].wait()
        part = pl.ds(piece * size, size)
        share[:, :, part] = dot(sorted_active, dec[:, part]).astype(bf16).reshape(latents, rows // latents, size)
        where = (slice(None), slice(None), part)
        copy = pltpu.make_async_copy(share.at[where], part_hbm.at[where], share_sems.at[piece])
        copy.start()
        share_copies.append(copy)
    for copy in share_copies:
        copy.wait()


def cut_decoder(own_segment, *refs):
    *_, dec_hbm, dec_out, dec, dec_part, dec_sems, out_sems = refs
    latents, _, own_cols = dec_out.shape
    size = dec.shape[1] // PIECES
    per_piece = latents // PIECES

    @pl.when(lax.axis_index("segment") == own_segment)
    def _():
        dec_copies = copies(dec_hbm, dec, dec_sems, 1)
        sent = copies(dec_part, dec_out, out_sems, 0)
        for copy in dec_copies:
            copy.start()
        for piece in range(PIECES):
            dec_copies[piece].wait()
            decoder = dec[:, pl.ds(piece * size, size)].astype(f32)
            for inner in range(per_piece):
                where = slice(inner * own_cols, (inner + 1) * own_cols)
                dec_part[piece * per_piece + inner] = decoder[:, where].astype(bf16)
            sent[piece].start()
        for copy in sent:
            copy.wait()


def cross_share(own_segment, *refs):
    active_ref, *_, cross_hbm, cross_out, cross, cross_part, cross_sems, out_sems = refs
    latents, _, own_cols = cross_out.shape
    size = cross.shape[1] // PIECES
    per_piece = latents // PIECES

    @pl.when(lax.axis_index("segment") == own_segment)
    def _():
        cross_copies = copies(cross_hbm, cross, cross_sems, 1)
        sent = copies(cross_part, cross_out, out_sems, 0)
        for copy in cross_copies:
            copy.start()
        earlier = active_ref[...]
        for piece in range(PIECES):
            cross_copies[piece].wait()
            share = dot(earlier, cross[:, pl.ds(piece * size, size)])
            for inner in range(per_piece):
                where = slice(inner * own_cols, (inner + 1) * own_cols)
                cross_part[piece * per_piece + inner] = share[:, where]
            sent[piece].start()
        for copy in sent:
            copy.wait()


def second_layer(dps, x_ref, recon_ref, bias_own, bias_other, list_own, list_other,
                 enc_own, enc_other, dec_hbm, cross_hbm, out_ref, enc, dec, cross, enc_sems, dec_sems, cross_sems):
    latents, some, cols = x_ref.shape
    rows = cross.shape[1]
    pair = some // dps
    group = rows // dps
    width = enc.shape[1]
    enc_copies = start_from(lax.axis_index("segment") == 0, enc_other, enc_own, enc, enc_sems, 0)
    dec_copies = copies(dec_hbm, dec, dec_sems, 0)
    cross_copies = copies(cross_hbm, cross, cross_sems, 0)
    half, tiles = list_own.shape[1] // 2, list_own.shape[2]
    segment = lax.axis_index("segment")
    is_first = segment == 0
    bias = jnp.where(is_first, bias_other[...], bias_own[...])
    size = cols // PIECES
    total = jnp.zeros((rows, width), f32)
    for piece in range(PIECES):
        enc_copies[piece].wait()
        dec_copies[piece].start()
        cross_copies[piece].start()
        part = pl.ds(piece * size, size)
        total += dot(x_ref[:, :, part].reshape(rows, size), enc[part, :])
    live = []
    for batch in range(half):
        both = [
            live_rows(is_first, list_other, list_own, segment * half + batch, tile, some // tiles, width)
            for tile in range(tiles)
        ]
        live += both * (latents // half)
    active = (jnp.maximum(total + bias, 0.0) * jnp.concatenate(live, axis=0)).astype(bf16)
    to_natural = one_hot(
        (rows, rows),
        lambda row: (row % group) // pair * some + row // group * pair + row % pair,
    )
    sorted_active = dot(to_natural, active).astype(bf16)
    for piece in range(latents):
        if piece % (latents // PIECES) == 0:
            dec_copies[piece // (latents // PIECES)].wait()
            cross_copies[piece // (latents // PIECES)].wait()
        share = folded(dot(sorted_active, dec[piece]) + cross[piece]).astype(bf16)
        recon = recon_ref[piece]
        extra = recon.shape[1] - LANES
        filled = share.shape[0]
        out_ref[piece, pl.ds(0, filled), :] = share
        out_ref[piece, pl.ds(filled, some), :] = recon[:, :LANES]
        out_ref[piece, pl.ds(filled + some, some), pl.ds(0, extra)] = recon[:, LANES:]
        out_ref[piece, pl.ds(filled + some, some), pl.ds(extra, LANES - extra)] = jnp.zeros((some, LANES - extra), bf16)


def take_own(x_ref, out_ref):
    count, group, padded = out_ref.shape
    half = x_ref.shape[0] // 2
    own_cols = x_ref.shape[2]
    segment = lax.axis_index("segment")
    for batch in range(half):
        mine = x_ref[segment * half + batch].astype(f32)
        mine = jnp.concatenate([mine, jnp.zeros((mine.shape[0], padded - own_cols), f32)], axis=1).astype(bf16)
        for piece in range(count):
            out_ref[piece, pl.ds(batch * mine.shape[0], mine.shape[0]), :] = mine


def repeat(own_cols, x_ref, out_ref):
    values = folded(x_ref[...].astype(f32)[:, :own_cols]).astype(bf16)
    for piece in range(out_ref.shape[0]):
        out_ref[piece] = values


def sum_parts(x_ref, out_ref):
    total = x_ref[0].astype(f32)
    for source in range(1, x_ref.shape[0]):
        total += x_ref[source].astype(f32)
    _, height, width = out_ref.shape
    per_row = total.shape[1] // width
    for piece in range(out_ref.shape[0]):
        down, across = divmod(piece, per_row)
        out_ref[piece] = total[down * height : (down + 1) * height, across * width : (across + 1) * width]


def sum_and_spread(x_ref, out_ref):
    total = x_ref[0]
    for source in range(1, x_ref.shape[0]):
        total += x_ref[source]
    rounded = total.astype(bf16).astype(f32)
    for piece in range(out_ref.shape[0]):
        out_ref[piece] = rounded


def add_and_normalize(pieces_ref, held_ref, gain_own, gain_other, out_ref, recon_ref, wide):
    count, height, width = pieces_ref.shape
    cols = wide.shape[1]
    per_row = cols // width
    for piece in range(count):
        down, across = divmod(piece, per_row)
        wide[pl.ds(down * height, height), pl.ds(across * width, width)] = pieces_ref[piece]
    recon = wide[...]
    own_cols = recon_ref.shape[2]
    for piece in range(recon_ref.shape[0]):
        recon_ref[piece] = recon[:, piece * own_cols : (piece + 1) * own_cols].astype(bf16)
    resid = (held_ref[...].astype(f32) + recon).astype(bf16).astype(f32)
    scaling = lax.rsqrt(jnp.mean(resid * resid, axis=1, keepdims=True) + norm_eps)
    gain = jnp.where(lax.axis_index("segment") == 0, gain_other[...], gain_own[...])
    normed = (resid * scaling * gain).astype(bf16)
    for piece in range(out_ref.shape[0]):
        out_ref[piece] = normed


def sum_for_dp(rows, dps, pair, x_ref, out_ref):
    latents = x_ref.shape[0]
    some = dps * pair
    filled = x_ref.shape[1] - 2 * some
    own_cols = out_ref.shape[3]
    extra = own_cols - LANES
    total = x_ref[0, pl.ds(0, filled), :].astype(f32)
    for source in range(1, latents):
        total += x_ref[source, pl.ds(0, filled), :].astype(f32)
    total = jnp.concatenate([total[:rows], right_part(total[rows:], extra)], axis=1)
    out_ref[1] = total.astype(bf16).reshape(dps, rows // dps, own_cols)
    dp = lax.axis_index("dp")
    choose_own = one_hot(
        (latents * pair, latents * some),
        lambda row: (row // pair) * some + dp * pair + row % pair,
    )
    left = x_ref[:, pl.ds(filled, some), :].reshape(latents * some, LANES)
    right = x_ref[:, pl.ds(filled + some, some), :].reshape(latents * some, LANES)
    recon = jnp.concatenate([dot(choose_own, left), dot(choose_own, right)[:, :extra]], axis=1).astype(bf16)
    for piece in range(dps):
        out_ref[0, piece] = recon


def finish(x_ref, out_ref):
    halves, dps = x_ref.shape[:2]
    is_first = lax.axis_index("segment") == 0
    dp = lax.axis_index("dp")
    for half in range(halves):
        total = x_ref[half, 0].astype(f32)
        for source in range(1, dps):
            total += x_ref[half, source].astype(f32)
        kept = x_ref[half, dp].astype(f32)
        out_ref[half] = jnp.where(is_first, kept, total).astype(bf16)


def call(kernel, outs, ins, scalars=0, hbm=0, scratch=(), limit=16, hbm_outs=0, aliases=None):
    vmem, far = pl.BlockSpec(memory_space=pltpu.VMEM), pl.BlockSpec(memory_space=pltpu.HBM)
    single = not isinstance(outs, (list, tuple))
    specs = [vmem] * (len(ins) - scalars - hbm)
    specs += [pl.BlockSpec(memory_space=pltpu.SMEM)] * scalars
    specs += [far] * hbm
    return pl.pallas_call(
        kernel,
        out_shape=outs,
        in_specs=specs,
        out_specs=vmem if single else [far] * hbm_outs + [vmem] * (len(outs) - hbm_outs),
        scratch_shapes=list(scratch),
        input_output_aliases=aliases or {},
        compiler_params=pltpu.CompilerParams(vmem_limit_bytes=limit * 1024 * 1024),
    )(*[placed(value, index, len(ins), hbm) for index, value in enumerate(ins)])


def placed(value, index, count, hbm):
    return pltpu.with_memory_space_constraint(value, pltpu.HBM) if index >= count - hbm else value


def array(shape, dtype=bf16, space=None):
    return jax.ShapeDtypeStruct(shape, dtype) if space is None else space(shape, dtype)


def body(resid_in, norm_gain, enc_weight, enc_bias, dec_self, dec_cross, block_ids, block_counts):
    is_first = lax.axis_index("segment") == 0
    latents = lax.axis_size("latent")
    dps = lax.axis_size("dp")
    batches, own_rows, own_cols = resid_in.shape
    cols = latents * own_cols
    width = enc_weight.shape[2]
    group = batches // 2 * own_rows
    some = dps * group // latents
    rows = group * dps
    padded = own_cols + -own_cols % 128

    enc_own, dec_own = enc_weight[0], dec_self[0]
    weights = [enc_own, swapped(enc_own), dec_own, swapped(dec_own)]
    gains = [norm_gain, swapped(norm_gain)]
    biases = [enc_bias, swapped(enc_bias)]
    slot = lax.broadcasted_iota(jnp.int32, block_ids.shape, block_ids.ndim - 1)
    listed = jnp.where(slot < block_counts[..., None], block_ids, -1)
    lists = [listed, swapped(listed)]

    def dp_first(resid):
        mine = call(take_own, array((dps, group, padded)), [resid])
        some_rows = exchanged(mine, "dp").reshape(rows, padded)
        every = call(functools.partial(repeat, own_cols), array((latents, rows * 7 // 4, LANES)), [some_rows])
        return exchanged(every, "latent").reshape(-1, LANES)

    def latent_first(resid):
        mine = call(take_own, array((latents, group, padded)), [resid])
        some_cols = exchanged(mine, "latent").reshape(latents * group, padded)
        every = call(
            functools.partial(repeat, own_cols), array((dps, latents * group * 7 // 4, LANES)), [some_cols]
        )
        return exchanged(every, "dp").reshape(-1, LANES)

    resid0 = lax.cond(is_first, dp_first, latent_first, resid_in)

    sems = pltpu.SemaphoreType.DMA((PIECES,))
    enc_space, dec_space = pltpu.VMEM(enc_own.shape, bf16), pltpu.VMEM(dec_own.shape, bf16)
    partial0, active0, held = call(
        functools.partial(first_layer, latents, dps),
        [array((latents, some, cols), space=pltpu.HBM), array((rows, width)), array((latents, some, own_cols))],
        [resid0] + gains + biases + lists + weights,
        scalars=2,
        hbm=4,
        scratch=[pltpu.VMEM((latents, rows, own_cols), bf16), enc_space, dec_space, pltpu.VMEM((latents, some, cols), bf16)] + [sems] * 3,
        limit=26,
        hbm_outs=1,
    )
    held = held.transpose(1, 0, 2).reshape(some, cols)
    dec_parts = pltpu.VMEM((latents, width, own_cols), bf16)
    cross_parts = pltpu.VMEM((latents, rows, own_cols), f32)
    out_sems = pltpu.SemaphoreType.DMA((PIECES,))
    dec_cut = array((latents, width, own_cols), space=pltpu.HBM)
    cut_space = dict(scratch=[dec_space, dec_parts, sems, out_sems], limit=24, hbm_outs=1)
    dec1 = call(functools.partial(cut_decoder, 1), [dec_cut], [dec_own], hbm=1, **cut_space)[0]
    cross_cut = array((latents, rows, own_cols), f32, space=pltpu.HBM)
    cross_space = dict(scratch=[dec_space, cross_parts, sems, out_sems], limit=24, hbm_outs=1)
    cross0 = call(functools.partial(cross_share, 1), [cross_cut], [active0, dec_cross], hbm=1, **cross_space)[0]
    partial0, dec1, cross0 = lax.optimization_barrier((partial0, dec1, cross0))
    dec1 = call(
        functools.partial(cut_decoder, 0), [dec_cut], [dec1, weights[3]], hbm=2, aliases={0: 0}, **cut_space
    )[0]
    cross0 = call(
        functools.partial(cross_share, 0), [cross_cut], [active0, cross0, dec_cross], hbm=2, aliases={1: 0}, **cross_space
    )[0]
    down = 2
    block = (dps, some // down, cols * down // dps)
    arrived = exchanged(partial0, "latent")
    arrived, held, dec1, cross0 = lax.optimization_barrier((arrived, held, dec1, cross0))
    share0 = call(sum_parts, array(block, f32), [arrived])
    recon0 = call(sum_and_spread, array(block, f32), [exchanged(share0, "dp")])
    normed1, recon0 = call(
        add_and_normalize,
        [array((latents, some, cols)), array((latents, some, own_cols))],
        [exchanged(recon0, "dp"), held] + gains,
        scratch=[pltpu.VMEM((some, cols), f32)],
    )
    normed1 = exchanged(normed1, "latent")

    outgoing = call(
        functools.partial(second_layer, dps),
        array((latents, rows * 7 // 4 + 2 * some, LANES)),
        [normed1, recon0] + biases + lists + weights[:2] + [dec1, cross0],
        scalars=2,
        hbm=4,
        scratch=[enc_space, dec_parts, cross_parts] + [sems] * 3,
        limit=32,
    )
    incoming = exchanged(outgoing, "latent")
    share1 = call(
        functools.partial(sum_for_dp, rows, dps, some // dps),
        array((2, dps, group, own_cols)),
        [incoming],
    )
    final = exchanged(share1.reshape(2 * dps, group, own_cols), ("segment", "dp"))
    result = call(finish, array((2, group, own_cols)), [final.reshape(2, dps, group, own_cols)])
    return result.reshape(1, batches, own_rows, own_cols)


def solution(mesh):
    return jax.shard_map(
        body,
        mesh=mesh,
        in_specs=(
            P(None, "dp", "latent"),
            P("segment", None),
            P("segment", None, ("latent", "dp")),
            P("segment", ("latent", "dp")),
            P("segment", ("latent", "dp"), None),
            P(("latent", "dp"), None),
            P("segment", None, None, ("latent", "dp"), None),
            P("segment", None, None, ("latent", "dp")),
        ),
        out_specs=P("segment", None, "dp", "latent"),
        check_vma=False,
    )
```
